32 devices in a mesh: seq: 16 (over z, y, x), head: 2 (over core).
Axes of the slice: x: 2, y: 2, z: 4, core: 2. Of those that a mesh axis runs over, the one named last changes fastest.
Arguments:
- block_input: bfloat16 [2048, 1024], P('seq'), may hold values from -7 to 7
- first_layer_value: bfloat16 [2048, 1024], P('seq', 'head'), may hold values from -6 to 6
- output_gradient: bfloat16 [2048, 1024], P('seq'), may hold values from -6 to 6
- segment_index: int32 [128], replicated, may hold values from 0 to 2, as said below
- channel_parameters: bfloat16 [11, 1024], P(None, 'seq'), may hold values from -1 to 1.5
- head_parameters: bfloat16 [8, 1024], P(None, ('head', 'seq')), may hold values from -11 to 3
- mixing_weights: bfloat16 [3, 1024, 1024], P(None, 'seq', 'head'), may hold values from -0.1875 to 0.1875
- output_weight: bfloat16 [1024, 1024], P('head', 'seq'), may hold values from -0.1875 to 0.1875
- low_rank_down_weight: bfloat16 [1024, 288], P('seq'), may hold values from -0.1875 to 0.1875
- low_rank_up_weight: bfloat16 [288, 1024], P(None, ('head', 'seq')), may hold values from -0.75 to 0.75
- channel_key_matrix: bfloat16 [1024, 4096], P('seq', 'head'), may hold values from -0.1875 to 0.1875
- channel_value_matrix: bfloat16 [4096, 1024], P('head', 'seq'), may hold values from -0.09375 to 0.09375
Outputs:
- block_out: bfloat16 [2048, 1024], P('seq')
- grad_block_in: float32 [2048, 1024], P('seq')
- grad_value_first: float32 [2048, 1024], P('seq', 'head')
- grad_chan_params: float32 [11, 1024], P(None, 'seq')
- grad_head_params: float32 [8, 1024], P(None, ('head', 'seq'))
- grad_mix_weights: float32 [3, 1024, 1024], P(None, 'seq', 'head')
- grad_out_weights: float32 [1024, 1024], P('head', 'seq')
- grad_lora_down: float32 [1024, 288], P('seq')
- grad_lora_up: float32 [288, 1024], P(None, ('head', 'seq'))
- grad_channel_key: float32 [1024, 4096], P('seq', 'head')
- grad_channel_value: float32 [4096, 1024], P('head', 'seq')
The draws below stay inside these ranges and needn't reach their ends.
Inputs may be any that keep to these rules, and one draw needn't show every extreme that they name: `segment_index`: ids never fall; ids 0 and 2 each hold at least one block and lie within the first and the last 8 blocks.
All inputs are finite; a program needn't handle non-finite values.
Results may differ from the reference program's by a relative error of at most 0.009.
The reference program's roundings to bfloat16 on the way count: a program that leaves them out, or rounds other values in their place, can miss the bound.
Values may be sent and summed in bfloat16 or wider, within the bound.
A program may use at most 256 MiB of HBM per device.

```python
import jax
import jax.numpy as jnp
from jax import lax

EMBED_DIM = 1024
FF = 4096
ATTEND_DIM = 64
DECAY_LOW_RANK = 64
RATE_RANK = 64
VALUE_RANK = 32
BLK = 16
TOK_DEV = 128
LOW_RANK_COLUMNS = 288
TOKENS = 2048


def draw_block_input(key, part):
    key = jax.random.fold_in(key, 41)
    lookup_vectors = jax.random.split(key, 2)
    common = jnp.clip(jax.random.normal(lookup_vectors[0], (EMBED_DIM,)), -3.0, 3.0)
    noise = jnp.clip(jax.random.normal(lookup_vectors[1], (TOKENS, EMBED_DIM)), -4.0, 4.0)
    weight = 0.8
    return (noise + weight * common[None, :]).astype(jnp.bfloat16)


def draw_segment_index(key, part):
    key = jax.random.fold_in(key, 11)
    per_device = TOK_DEV // BLK
    block_count = TOKENS // BLK
    first_key, second_key = jax.random.split(key)
    head_cut = jax.random.randint(first_key, (), 1, per_device)
    tail_cut = block_count - jax.random.randint(second_key, (), 1, per_device)
    position = jnp.arange(block_count)
    return (position >= head_cut).astype(jnp.int32) + (position >= tail_cut).astype(jnp.int32)


def draw_channel_parameters(key, part):
    key = jax.random.fold_in(key, 21)
    lookup_vectors = jax.random.split(key, 3)
    gains = 1.0 + 0.2 * jnp.clip(jax.random.normal(lookup_vectors[0], (2, EMBED_DIM)), -2.0, 2.0)
    biases = 0.3 * jnp.clip(jax.random.normal(lookup_vectors[1], (2, EMBED_DIM)), -3.0, 3.0)
    coeffs = jax.random.uniform(lookup_vectors[2], (7, EMBED_DIM))
    piled_vectors = jnp.concatenate([gains[0:1], biases[0:1], gains[1:2], biases[1:2], coeffs], axis=0)
    return piled_vectors.astype(jnp.bfloat16)


def draw_head_parameters(key, part):
    key = jax.random.fold_in(key, 31)
    lookup_vectors = jax.random.split(key, 9)
    attend_count = EMBED_DIM // ATTEND_DIM
    slow_share = 0.5
    rate_low_end = -2.0
    rate_high_end = 2.0
    slow_heads = jax.random.uniform(lookup_vectors[0], (attend_count,)) < slow_share
    slow_level = jax.random.uniform(lookup_vectors[1], (attend_count,), minval=-10.5, maxval=-9.0)
    fast_level = jax.random.uniform(lookup_vectors[2], (attend_count,), minval=-4.0, maxval=-2.5)
    forget_shift = jnp.repeat(jnp.where(slow_heads, slow_level, fast_level), ATTEND_DIM) + jax.random.uniform(lookup_vectors[3], (EMBED_DIM,), minval=-0.5, maxval=0.5)
    learning_shift = jax.random.uniform(lookup_vectors[4], (EMBED_DIM,), minval=rate_low_end, maxval=rate_high_end)
    payload_shift = jnp.clip(jax.random.normal(lookup_vectors[5], (EMBED_DIM,)), -3.0, 3.0)
    lookup_gain_vectors = jax.random.uniform(lookup_vectors[6], (2, EMBED_DIM), minval=0.5, maxval=1.5)
    extra_coefficient = 0.5 * jnp.clip(jax.random.normal(lookup_vectors[7], (EMBED_DIM,)), -3.0, 3.0)
    vector_length = jax.random.uniform(lookup_vectors[8], (2, EMBED_DIM), minval=0.5, maxval=1.5)
    vector_length = vector_length.at[1].set(vector_length[1] - 1.0)
    piled_vectors = jnp.stack([forget_shift, learning_shift, payload_shift, lookup_gain_vectors[0], lookup_gain_vectors[1], extra_coefficient, vector_length[0], vector_length[1]])
    return piled_vectors.astype(jnp.bfloat16)


def block_scale(key, dims, shards, smallest, largest):
    level, own = 1.0, jax.random.fold_in(key, 6)
    for dim, blocks in shards:
        draws = jnp.exp(jax.random.uniform(jax.random.fold_in(own, dim), (blocks,), jnp.float32, smallest / len(shards), largest / len(shards)))
        level = level * jnp.repeat(draws, dims[dim] // blocks).reshape([-1 if axis == dim else 1 for axis in range(len(dims))])
    return level


def centred(rng, dims, deviation, limit, cuts=(), held_as=jnp.bfloat16):
    drawn = deviation * jax.random.normal(rng, dims, jnp.float32)
    if cuts:
        drawn = drawn * block_scale(rng, dims, cuts, -0.22, 0.18)
    return jnp.clip(drawn, -limit, limit).astype(held_as)


def setup_inputs(seed: int = 0) -> dict:
    key_list = jax.random.split(jax.random.key(seed), 13)
    block_input = draw_block_input(jax.random.fold_in(key_list[12], 71), 0)
    first_layer_value = centred(key_list[1], (TOKENS, EMBED_DIM), 1.0, 6.0, ((0, 16), (1, 2)))
    output_gradient = centred(key_list[2], (TOKENS, EMBED_DIM), 1.0, 6.0, ((0, 16),))
    segment_index = draw_segment_index(jax.random.fold_in(key_list[12], 71), 0)
    channel_parameters = draw_channel_parameters(jax.random.fold_in(key_list[12], 71), 0)
    head_parameters = draw_head_parameters(jax.random.fold_in(key_list[12], 71), 0)
    mixing_weights = centred(key_list[6], (3, EMBED_DIM, EMBED_DIM), EMBED_DIM ** -0.5, 0.1875, ((1, 16), (2, 2)))
    output_weight = centred(key_list[7], (EMBED_DIM, EMBED_DIM), EMBED_DIM ** -0.5, 0.1875, ((0, 2), (1, 16)))
    low_rank_down_weight = centred(key_list[8], (EMBED_DIM, LOW_RANK_COLUMNS), EMBED_DIM ** -0.5, 0.1875, ((0, 16),))
    low_rank_up_weight = centred(key_list[9], (LOW_RANK_COLUMNS, EMBED_DIM), DECAY_LOW_RANK ** -0.5, 0.75, ((1, 32),))
    channel_key_matrix = centred(key_list[10], (EMBED_DIM, FF), EMBED_DIM ** -0.5, 0.1875, ((0, 16), (1, 2)))
    channel_value_matrix = centred(key_list[11], (FF, EMBED_DIM), FF ** -0.5, 0.09375, ((0, 2), (1, 16)))
    return dict(block_input=block_input, first_layer_value=first_layer_value, output_gradient=output_gradient, segment_index=segment_index, channel_parameters=channel_parameters, head_parameters=head_parameters, mixing_weights=mixing_weights, output_weight=output_weight, low_rank_down_weight=low_rank_down_weight, low_rank_up_weight=low_rank_up_weight, channel_key_matrix=channel_key_matrix, channel_value_matrix=channel_value_matrix)


PRECISE = lax.Precision.HIGHEST

@jax.custom_vjp
def lowrank_hidden(v):
    return lax.optimization_barrier(v.astype(jnp.bfloat16)).astype(jnp.float32)

@jax.custom_vjp
def low_back(v):
    return v

def low_keep(v):
    return (lowrank_hidden(v), None)

def low_pass(kept, grad):
    return (grad,)

def back_keep(v):
    return (v, None)

def back_low(kept, grad):
    return (lowrank_hidden(grad),)
lowrank_hidden.defvjp(low_keep, low_pass)
low_back.defvjp(back_keep, back_low)

def matrix_multiply(operand, weights):
    return low_back(jnp.dot(operand, weights, precision=PRECISE))

def layer_norm(value_rows, scale_vec, offset_vec):
    centre = value_rows - lax.optimization_barrier(jnp.mean(value_rows, axis=-1, keepdims=True))
    spread = lax.optimization_barrier(jnp.mean(centre * centre, axis=-1, keepdims=True))
    return centre * lax.rsqrt(spread + 1e-05) * scale_vec + offset_vec

def previous_rows(value_rows, start_rows):
    moved = jnp.concatenate([jnp.zeros_like(value_rows[:1]), value_rows[:-1]], axis=0)
    return moved * (1.0 - start_rows)[:, None]

def token_starts(segment_index):
    changed = jnp.concatenate([jnp.ones((1,), jnp.float32), (segment_index[1:] != segment_index[:-1]).astype(jnp.float32)])
    others = jnp.zeros((segment_index.shape[0], BLK - 1), jnp.float32)
    return jnp.concatenate([changed[:, None], others], axis=1).reshape(-1)

def prepare_inputs(receptance_unscaled, key_unscaled, value_unscaled, decay_low_rank, rate_low_rank, value_low_rank, first_layer_value, attend_elements):
    rows_here = receptance_unscaled.shape[0]
    attend_count = receptance_unscaled.shape[1] // ATTEND_DIM
    logarithm_scale = -jax.nn.softplus(-(attend_elements[0] + decay_low_rank)) - 0.5
    log_decay = -jnp.exp(logarithm_scale)
    rate_sigmoid = jax.nn.sigmoid(attend_elements[1] + rate_low_rank)
    payload_blended = value_unscaled + (first_layer_value - value_unscaled) * jax.nn.sigmoid(attend_elements[2] + value_low_rank)
    scaled = (key_unscaled * attend_elements[3]).reshape(rows_here, attend_count, ATTEND_DIM)
    unit_key = scaled * lax.rsqrt(lax.optimization_barrier(jnp.sum(scaled * scaled, axis=-1, keepdims=True)) + 1e-05)
    lookup_used = key_unscaled * (1.0 + (rate_sigmoid - 1.0) * attend_elements[4])
    layout = (rows_here, attend_count, ATTEND_DIM)
    return (receptance_unscaled.reshape(layout), log_decay.reshape(layout), -unit_key, unit_key * rate_sigmoid.reshape(layout), lookup_used.reshape(layout), payload_blended.reshape(layout))

def finish(read_out, reader_vectors, lookup_used, payload_blended, gate_activation, attend_elements):
    rows_here, attend_count, _ = read_out.shape
    centre = read_out - lax.optimization_barrier(jnp.mean(read_out, axis=-1, keepdims=True))
    unit_length_vectors = centre * lax.rsqrt(lax.optimization_barrier(jnp.mean(centre * centre, axis=-1, keepdims=True)) + 0.00064)
    extra_addend = lax.optimization_barrier(jnp.sum(reader_vectors * lookup_used * attend_elements[5].reshape(attend_count, ATTEND_DIM), axis=-1, keepdims=True)) * payload_blended
    final_answer = unit_length_vectors * attend_elements[6].reshape(attend_count, ATTEND_DIM) + attend_elements[7].reshape(attend_count, ATTEND_DIM) + extra_addend
    return final_answer.reshape(rows_here, attend_count * ATTEND_DIM) * gate_activation

def token_step(memory, inputs_now):
    recv_now, decay_now, removal_now, refill_now, key_now, value_now, start_now = inputs_now
    memory = memory * (1.0 - start_now)
    removed = lax.optimization_barrier(jnp.sum(memory * removal_now[:, None, :], axis=2))
    memory = memory * jnp.exp(decay_now)[:, None, :] + removed[:, :, None] * refill_now[:, None, :] + value_now[:, :, None] * key_now[:, None, :]
    return (memory, lax.optimization_barrier(jnp.sum(memory * recv_now[:, None, :], axis=2)))

def block_step(memory, inputs_now):
    return lax.scan(token_step, memory, inputs_now)

def recurrence(reader_vectors, log_decay, removal, refill, lookup_used, payload_blended, start_rows):
    rows_here, attend_count, head_width = reader_vectors.shape
    block_count = rows_here // BLK
    feeds = tuple((value_rows.reshape(block_count, BLK, attend_count, head_width) for value_rows in (reader_vectors, log_decay, removal, refill, lookup_used, payload_blended)))
    feeds = feeds + (start_rows.reshape(block_count, BLK),)
    memory = jnp.zeros((attend_count, head_width, head_width), jnp.float32)
    _, outputs = lax.scan(jax.checkpoint(block_step), memory, feeds)
    return outputs.reshape(rows_here, attend_count, head_width)

def forward_pass(block_input, first_layer_value, channel_parameters, head_parameters, mixing_weights, output_weight, low_rank_down_weight, low_rank_up_weight, channel_key_matrix, channel_value_matrix, start_rows):
    first_boundary = DECAY_LOW_RANK
    second_boundary = first_boundary + RATE_RANK
    third_boundary = second_boundary + VALUE_RANK
    norm_one = layer_norm(block_input, channel_parameters[0], channel_parameters[1])
    shift_one = previous_rows(norm_one, start_rows) - norm_one
    recv_in, decay_input, key_in, value_input, rate_input, gate_input = [lowrank_hidden(norm_one + shift_one * channel_parameters[4 + number]) for number in range(6)]
    receptance_unscaled = matrix_multiply(recv_in, mixing_weights[0])
    key_unscaled = matrix_multiply(key_in, mixing_weights[1])
    value_unscaled = matrix_multiply(value_input, mixing_weights[2])
    decay_lowrank_output = matrix_multiply(decay_input, low_rank_down_weight[:, :first_boundary])
    rate_lowrank_output = matrix_multiply(rate_input, low_rank_down_weight[:, first_boundary:second_boundary])
    value_lowrank_output = matrix_multiply(value_input, low_rank_down_weight[:, second_boundary:third_boundary])
    gate_lowrank_output = matrix_multiply(gate_input, low_rank_down_weight[:, third_boundary:])
    decay_low_rank = matrix_multiply(lowrank_hidden(jnp.tanh(decay_lowrank_output)), low_rank_up_weight[:first_boundary])
    rate_low_rank = matrix_multiply(lowrank_hidden(rate_lowrank_output), low_rank_up_weight[first_boundary:second_boundary])
    value_low_rank = matrix_multiply(lowrank_hidden(value_lowrank_output), low_rank_up_weight[second_boundary:third_boundary])
    gate_activation = matrix_multiply(lowrank_hidden(jax.nn.sigmoid(gate_lowrank_output)), low_rank_up_weight[third_boundary:])
    prepared_inputs = prepare_inputs(receptance_unscaled, key_unscaled, value_unscaled, decay_low_rank, rate_low_rank, value_low_rank, first_layer_value, head_parameters)
    read_out = recurrence(*prepared_inputs, start_rows)
    mixed_out = lowrank_hidden(finish(read_out, prepared_inputs[0], prepared_inputs[4], prepared_inputs[5], gate_activation, head_parameters))
    hidden_in = block_input + matrix_multiply(mixed_out, output_weight)
    norm_two = layer_norm(hidden_in, channel_parameters[2], channel_parameters[3])
    key_two = lowrank_hidden(norm_two + (previous_rows(norm_two, start_rows) - norm_two) * channel_parameters[10])
    activated = lowrank_hidden(jnp.square(jax.nn.relu(matrix_multiply(key_two, channel_key_matrix))))
    return hidden_in + matrix_multiply(activated, channel_value_matrix)

def reference(block_input, first_layer_value, output_gradient, segment_index, channel_parameters, head_parameters, mixing_weights, output_weight, low_rank_down_weight, low_rank_up_weight, channel_key_matrix, channel_value_matrix):
    start_rows = token_starts(segment_index)
    float_values = tuple((value_rows.astype(jnp.float32) for value_rows in (block_input, first_layer_value, channel_parameters, head_parameters, mixing_weights, output_weight, low_rank_down_weight, low_rank_up_weight, channel_key_matrix, channel_value_matrix)))

    def wrapped(*params):
        return forward_pass(*params, start_rows)
    final_answer, pullback = jax.vjp(wrapped, *float_values)
    grads = pullback(output_gradient.astype(jnp.float32))
    return (final_answer.astype(jnp.bfloat16), grads[0], grads[1], grads[2], grads[3], grads[4], grads[5], grads[6], grads[7], grads[8], grads[9])
```

```python
from functools import partial

import jax
import jax.numpy as jnp
from jax import lax
from jax.sharding import PartitionSpec as P

ATTEND_DIM = 64
DECAY_LOW_RANK = 64
RATE_RANK = 64
VALUE_RANK = 32
BLK = 16


PRECISE = lax.Precision.HIGHEST
FINE = lax.Precision.HIGH


def from_behind(value, axis, steps):
    count = lax.axis_size(axis)
    initial, last = (max(0, -steps), min(count, count - steps))
    return lax.ppermute(value, axis, [(source, source + steps) for source in range(initial, last)])


def swap_sum(value):
    return value + lax.ppermute(value, "head", [(0, 1), (1, 0)])


def times(left, right, turned=False):
    shape = "hij,hkj->hik" if turned else "hij,hjk->hik"
    return jnp.einsum(shape, left, right, precision=FINE)


def chain_steps(count):
    return [1 << power for power in range((count - 1).bit_length())]


def exclusive_maps(own_map, direction):
    count = lax.axis_size("seq")
    place = lax.axis_index("seq")
    behind = place if direction > 0 else count - 1 - place
    maps = []
    total = own_map
    for step in chain_steps(count):
        maps.append(total)
        if 2 * step < count:
            arrived = from_behind(total, "seq", direction * step)
            total = jnp.where(behind >= step, times(arrived, total), total)
    return maps


def exclusive_chain(maps, own_add, direction):
    total = own_add
    for step, step_map in zip(chain_steps(lax.axis_size("seq")), maps):
        arrived = from_behind(total, "seq", direction * step)
        total = total + times(arrived, step_map)
    return from_behind(total, "seq", direction)


def halve_sum(rows, sent_type, order):
    count = lax.axis_size("seq")
    place = lax.axis_index("seq")
    bits = (count - 1).bit_length()
    left = list(range(bits - 1, -1, -1))
    held = rows.reshape((2,) * bits + (rows.shape[0] // count, rows.shape[1]))
    for bit in [number for number in order if number < bits] + list(range(len(order), bits)):
        where = left.index(bit)
        left.remove(bit)
        mine = (place >> bit) & 1
        kept = lax.dynamic_index_in_dim(held, mine, where, False)
        sent = lax.dynamic_index_in_dim(held, 1 - mine, where, False).astype(sent_type)
        pairs = [(number, number ^ (1 << bit)) for number in range(count)]
        held = kept.astype(jnp.float32) + lax.ppermute(sent, "seq", pairs).astype(jnp.float32)
    return held


def halves_side_by_side(rows, width):
    columns = rows.shape[1] // 2
    cut = rows.reshape(-1, width, 2 * columns)
    return jnp.concatenate([cut[:, :, :columns], cut[:, :, columns:]], axis=1).reshape(-1, columns)


def halves_stacked(rows, width):
    columns = rows.shape[1]
    cut = rows.reshape(-1, 2 * width, columns)
    return jnp.concatenate([cut[:, :width], cut[:, width:]], axis=2).reshape(-1, 2 * columns)


def product_matrix(operand, weights):
    return jnp.dot(operand, weights, preferred_element_type=jnp.float32)


def back_product(gradient, weights):
    return lax.dot_general(
        gradient, weights, (((1,), (1,)), ((), ())), preferred_element_type=jnp.float32
    )


def weight_grad(operand, gradient):
    return lax.dot_general(
        operand, gradient, (((0,), (0,)), ((), ())), preferred_element_type=jnp.float32
    )


def layer_norm(value_rows, scale_vec, offset_vec):
    centre = value_rows - jnp.mean(value_rows, axis=-1, keepdims=True)
    spread = jnp.mean(centre * centre, axis=-1, keepdims=True)
    return centre * lax.rsqrt(spread + 1e-05) * scale_vec + offset_vec


def prepare_inputs(
    receptance_unscaled,
    key_unscaled,
    value_unscaled,
    decay_low_rank,
    rate_low_rank,
    value_low_rank,
    first_layer_value,
    attend_elements,
):
    rows_here = receptance_unscaled.shape[0]
    attend_count = receptance_unscaled.shape[1] // ATTEND_DIM
    logarithm_scale = -jax.nn.softplus(-(attend_elements[0] + decay_low_rank)) - 0.5
    log_decay = -jnp.exp(logarithm_scale)
    rate_sigmoid = jax.nn.sigmoid(attend_elements[1] + rate_low_rank)
    payload_blended = value_unscaled + (first_layer_value - value_unscaled) * jax.nn.sigmoid(
        attend_elements[2] + value_low_rank
    )
    scaled = (key_unscaled * attend_elements[3]).reshape(rows_here, attend_count, ATTEND_DIM)
    unit_key = scaled * lax.rsqrt(jnp.sum(scaled * scaled, axis=-1, keepdims=True) + 1e-05)
    lookup_used = key_unscaled * (1.0 + (rate_sigmoid - 1.0) * attend_elements[4])
    layout = (rows_here, attend_count, ATTEND_DIM)
    return (
        receptance_unscaled.reshape(layout),
        log_decay.reshape(layout),
        -unit_key,
        unit_key * rate_sigmoid.reshape(layout),
        lookup_used.reshape(layout),
        payload_blended.reshape(layout),
    )


def finish(
    read_out, reader_vectors, lookup_used, payload_blended, gate_activation, attend_elements
):
    rows_here, attend_count, _ = read_out.shape
    centre = read_out - jnp.mean(read_out, axis=-1, keepdims=True)
    unit_length_vectors = centre * lax.rsqrt(
        jnp.mean(centre * centre, axis=-1, keepdims=True) + 0.00064
    )
    extra_addend = (
        jnp.sum(
            reader_vectors * lookup_used * attend_elements[5].reshape(attend_count, ATTEND_DIM),
            axis=-1,
            keepdims=True,
        )
        * payload_blended
    )
    final_answer = (
        unit_length_vectors * attend_elements[6].reshape(attend_count, ATTEND_DIM)
        + attend_elements[7].reshape(attend_count, ATTEND_DIM)
        + extra_addend
    )
    return final_answer.reshape(rows_here, attend_count * ATTEND_DIM) * gate_activation


@jax.custom_vjp
def unit_inverse(strict_part):
    unit = jnp.eye(strict_part.shape[-1], dtype=jnp.float32)[None]
    inverse = unit + strict_part
    power = strict_part
    for _ in range(BLK.bit_length() - 2):
        power = times(power, power)
        inverse = inverse + times(inverse, power)
    return inverse


def unit_inverse_keep(strict_part):
    inverse = unit_inverse(strict_part)
    return inverse, inverse


def unit_inverse_pull(inverse, gradient):
    turned = jnp.swapaxes(inverse, 1, 2)
    return (times(times(turned, gradient), turned),)


unit_inverse.defvjp(unit_inverse_keep, unit_inverse_pull)


def chunk_terms(reader_vectors, log_decay, removal, refill, lookup_used, payload_blended, keep):
    rows_here, attend_count, head_width = reader_vectors.shape
    block_count = rows_here // BLK
    recv, decay, removal, refill, lookup, payload = [
        jnp.transpose(rows, (1, 0, 2))
        for rows in (reader_vectors, log_decay, removal, refill, lookup_used, payload_blended)
    ]
    token = jnp.arange(rows_here)
    same = (token[:, None] // BLK) == (token[None, :] // BLK)
    strict = (same & (token[:, None] > token[None, :])).astype(jnp.float32)
    inclusive = (same & (token[:, None] >= token[None, :])).astype(jnp.float32)

    def blocks(rows):
        return rows.reshape(attend_count, block_count, BLK, head_width)

    cumulative = jnp.einsum("ts,hsj->htj", inclusive, decay, precision=PRECISE)
    growth = jnp.exp(-cumulative)
    refill_grown = refill * growth
    key_grown = lookup * growth
    first_term = removal * jnp.exp(cumulative - decay)
    reader_term = recv * jnp.exp(cumulative)
    mix_refill = times(first_term, refill_grown, True) * strict
    mix_key = times(first_term, key_grown, True) * strict
    read_refill = times(reader_term, refill_grown, True) * inclusive
    read_key = times(reader_term, key_grown, True) * inclusive
    inverse = unit_inverse(mix_refill)
    removed_map = times(inverse, first_term)
    removed_add = times(inverse, times(mix_key, payload))
    read_map = reader_term + times(read_refill, removed_map)
    read_add = times(read_refill, removed_add) + times(read_key, payload)
    total = blocks(cumulative)[:, :, BLK - 1 :]
    tail = jnp.exp(total - blocks(cumulative))
    refill_tail = blocks(refill) * tail
    key_tail = blocks(lookup) * tail

    def outer(left, right):
        return jnp.einsum("hcti,hctj->chij", blocks(left), right, precision=FINE)

    unit = jnp.eye(head_width, dtype=jnp.float32)
    kept = keep[:, None, None, None]
    decayed = jnp.exp(jnp.transpose(total, (1, 0, 2, 3)))
    state_map = (unit * decayed + outer(removed_map, refill_tail)) * kept
    state_add = outer(removed_add, refill_tail) + outer(payload, key_tail)
    return state_map, state_add, blocks(read_map) * keep[None, :, None, None], read_add


def shards(
    block_input,
    first_layer_value,
    output_gradient,
    segment_index,
    channel_parameters,
    head_parameters,
    mixing_weights,
    output_weight,
    low_rank_down_weight,
    low_rank_up_weight,
    channel_key_matrix,
    channel_value_matrix,
):
    width = low_rank_down_weight.shape[0]
    half = low_rank_up_weight.shape[1]
    hidden_local = mixing_weights.shape[2]
    low_columns = low_rank_down_weight.shape[1]
    head_rows = head_parameters.shape[0]
    own_columns = jnp.concatenate([low_rank_up_weight, head_parameters], axis=0).T
    first_pack = jnp.concatenate(
        [
            mixing_weights[0],
            mixing_weights[1],
            mixing_weights[2],
            low_rank_down_weight,
            halves_side_by_side(own_columns, half),
            channel_parameters.T,
        ],
        axis=1,
    )
    first_full = lax.all_gather(first_pack, "seq", axis=0, tiled=True)
    later_pack = jnp.concatenate(
        [output_weight.T, channel_key_matrix, channel_value_matrix.T], axis=1
    )
    later_full = lax.all_gather(later_pack, "seq", axis=0, tiled=True)
    mix_full = [
        first_full[:, number * hidden_local : (number + 1) * hidden_local] for number in range(3)
    ]
    place_down = 3 * hidden_local
    place_up = place_down + low_columns
    place_chan = place_up + (low_columns + head_rows) // 2
    down_full = first_full[:, place_down:place_up]
    columns_full = halves_stacked(first_full[:, place_up:place_chan], half)
    up_turned = columns_full[:, :low_columns]
    head_full = columns_full[:, low_columns:].T
    chan_full = first_full[:, place_chan:].T
    units = channel_key_matrix.shape[1]
    out_turned = later_full[:, :hidden_local]
    key_full = later_full[:, hidden_local : hidden_local + units]
    value_turned = later_full[:, hidden_local + units :]
    chan_vals = chan_full.astype(jnp.float32)
    attend_elements = head_full.astype(jnp.float32)
    first_boundary = DECAY_LOW_RANK
    second_boundary = first_boundary + RATE_RANK
    third_boundary = second_boundary + VALUE_RANK
    rows_here = block_input.shape[0]
    attend_count = head_full.shape[1] // ATTEND_DIM
    block_count = rows_here // BLK
    place = lax.axis_index("seq")
    earlier_id = jnp.where(
        place > 0,
        lax.dynamic_slice_in_dim(segment_index, jnp.maximum(place * block_count - 1, 0), 1),
        -1,
    )
    own_ids = lax.dynamic_slice_in_dim(segment_index, place * block_count, block_count)
    block_starts = (own_ids != jnp.concatenate([earlier_id, own_ids[:-1]])).astype(jnp.float32)
    keep_block = 1.0 - block_starts
    keep_token = jnp.concatenate(
        [keep_block[:, None], jnp.ones((block_count, BLK - 1), jnp.float32)], axis=1
    ).reshape(-1)
    x_input = block_input.astype(jnp.float32)
    norm_one, norm_one_pull = jax.vjp(layer_norm, x_input, chan_vals[0], chan_vals[1])
    edge_one = from_behind(norm_one[rows_here - 1 :], "seq", 1)
    shift_one = jnp.concatenate([edge_one, norm_one[:-1]], axis=0) * keep_token[:, None] - norm_one
    recv_in, decay_input, key_in, value_input, rate_input, gate_input = [
        (norm_one + shift_one * chan_vals[4 + number]).astype(jnp.bfloat16) for number in range(6)
    ]
    receptance_unscaled = product_matrix(recv_in, mix_full[0])
    key_unscaled = product_matrix(key_in, mix_full[1])
    value_unscaled = product_matrix(value_input, mix_full[2])
    decay_lowrank_output = product_matrix(decay_input, down_full[:, :first_boundary])
    rate_lowrank_output = product_matrix(rate_input, down_full[:, first_boundary:second_boundary])
    value_lowrank_output = product_matrix(value_input, down_full[:, second_boundary:third_boundary])
    gate_lowrank_output = product_matrix(gate_input, down_full[:, third_boundary:])
    decay_hidden = jnp.tanh(decay_lowrank_output).astype(jnp.bfloat16)
    rate_hidden = rate_lowrank_output.astype(jnp.bfloat16)
    value_hidden = value_lowrank_output.astype(jnp.bfloat16)
    gate_sig = jax.nn.sigmoid(gate_lowrank_output)
    gate_hid = gate_sig.astype(jnp.bfloat16)
    decay_low_rank = back_product(decay_hidden, up_turned[:, :first_boundary])
    rate_low_rank = back_product(rate_hidden, up_turned[:, first_boundary:second_boundary])
    value_low_rank = back_product(
        value_hidden, up_turned[:, second_boundary:third_boundary]
    )
    gate_activation = back_product(gate_hid, up_turned[:, third_boundary:])
    first_values = first_layer_value.astype(jnp.float32)
    prepared_inputs, prepare_pull = jax.vjp(
        prepare_inputs,
        receptance_unscaled,
        key_unscaled,
        value_unscaled,
        decay_low_rank,
        rate_low_rank,
        value_low_rank,
        first_values,
        attend_elements,
    )
    (state_map, state_add, read_map, read_add), local_pull = jax.vjp(
        partial(chunk_terms, keep=keep_block), *prepared_inputs
    )
    before_map, before_add = [None], [None]
    run_map, run_add = state_map[0], state_add[0]
    for number in range(1, block_count):
        before_map.append(run_map)
        before_add.append(run_add)
        run_add = times(run_add, state_map[number]) + state_add[number]
        run_map = times(run_map, state_map[number])
    after_map = [state_map[block_count - 1]]
    for number in range(block_count - 2, -1, -1):
        after_map.append(times(state_map[number], after_map[-1]))
    after_map = after_map[::-1]
    forward_maps = exclusive_maps(run_map, 1)
    backward_maps = exclusive_maps(jnp.swapaxes(run_map, 1, 2), -1)
    start_state = exclusive_chain(forward_maps, run_add, 1)
    states = jnp.concatenate(
        [
            start_state[None],
            jnp.einsum("hij,chjk->chik", start_state, jnp.stack(before_map[1:]), precision=FINE)
            + jnp.stack(before_add[1:]),
        ],
        axis=0,
    )
    read_out = jnp.transpose(
        jnp.einsum("hctj,chij->hcti", read_map, states, precision=FINE).reshape(read_add.shape)
        + read_add,
        (1, 0, 2),
    )
    mixed_f, finish_pull = jax.vjp(
        finish,
        read_out,
        prepared_inputs[0],
        prepared_inputs[4],
        prepared_inputs[5],
        gate_activation,
        attend_elements,
    )
    mixed_low = mixed_f.astype(jnp.bfloat16)
    hidden_in = x_input + swap_sum(back_product(mixed_low, out_turned))
    norm_two, norm_two_pull = jax.vjp(layer_norm, hidden_in, chan_vals[2], chan_vals[3])
    edge_two = from_behind(norm_two[rows_here - 1 :], "seq", 1)
    shift_two = jnp.concatenate([edge_two, norm_two[:-1]], axis=0) * keep_token[:, None] - norm_two
    key_two = (norm_two + shift_two * chan_vals[10]).astype(jnp.bfloat16)
    pre_act = product_matrix(key_two, key_full)
    activated = jnp.square(jax.nn.relu(pre_act)).astype(jnp.bfloat16)
    block_out = hidden_in + swap_sum(back_product(activated, value_turned))
    grad_output = output_gradient.astype(jnp.float32)
    grad_ffo = grad_output.astype(jnp.bfloat16)
    value_sum = halve_sum(weight_grad(grad_ffo, activated), jnp.bfloat16, (1, 0, 3, 2))
    grad_pre = (product_matrix(grad_ffo, value_turned) * 2.0 * jax.nn.relu(pre_act)).astype(
        jnp.bfloat16
    )
    key_sum = halve_sum(weight_grad(key_two, grad_pre), jnp.bfloat16, (0, 1, 3, 2))
    part_key_two = back_product(grad_pre, key_full)
    grad_key_two = swap_sum(part_key_two)
    grad_coeff_two = jnp.sum(grad_key_two * shift_two, axis=0)
    toward_two = grad_key_two * chan_vals[10] * keep_token[:, None]
    back_two = from_behind(toward_two[:1], "seq", -1)
    grad_norm_two = grad_key_two * (1.0 - chan_vals[10]) + jnp.concatenate(
        [toward_two[1:], back_two], axis=0
    )
    grad_hidden, grad_gain_two, grad_bias_two = norm_two_pull(grad_norm_two)
    grad_hidden = grad_hidden + grad_output
    grad_attn = grad_hidden.astype(jnp.bfloat16)
    out_sum = halve_sum(weight_grad(grad_attn, mixed_low), jnp.bfloat16, (1, 0, 3, 2))
    grad_mixed = product_matrix(grad_attn, out_turned)
    grad_read, grad_recv_a, grad_key_a, grad_value_a, grad_gate, grad_head_a = finish_pull(
        grad_mixed
    )
    read_turned = jnp.transpose(grad_read, (1, 0, 2))
    read_blocks = read_turned.reshape(read_map.shape)
    grad_states = jnp.einsum("hcti,hctj->chij", read_blocks, read_map, precision=FINE)
    run_grad = grad_states[block_count - 1]
    after_grad = [jnp.zeros_like(run_grad), run_grad]
    for number in range(block_count - 2, -1, -1):
        run_grad = grad_states[number] + times(run_grad, state_map[number], True)
        after_grad.append(run_grad)
    after_grad = jnp.stack(after_grad[block_count - 1 :: -1])
    grad_end = exclusive_chain(backward_maps, run_grad, -1)
    grad_add = after_grad + jnp.concatenate(
        [
            jnp.einsum("hij,chkj->chik", grad_end, jnp.stack(after_map[1:]), precision=FINE),
            grad_end[None],
        ],
        axis=0,
    )
    grad_map = jnp.einsum("chij,chik->chjk", states, grad_add, precision=FINE)
    grad_read_map = jnp.einsum("hcti,chij->hctj", read_blocks, states, precision=FINE)
    chain_grads = local_pull((grad_map, grad_add, grad_read_map, read_turned))
    cotangents = (
        grad_recv_a + chain_grads[0],
        chain_grads[1],
        chain_grads[2],
        chain_grads[3],
        grad_key_a + chain_grads[4],
        grad_value_a + chain_grads[5],
    )
    (
        grad_recv_raw,
        grad_key_raw,
        grad_value_raw,
        gradient_decay_low_rank,
        gradient_rate_low_rank,
        gradient_value_low_rank,
        grad_first,
        grad_head_b,
    ) = prepare_pull(cotangents)
    recv_round = grad_recv_raw.astype(jnp.bfloat16)
    key_round = grad_key_raw.astype(jnp.bfloat16)
    value_round = grad_value_raw.astype(jnp.bfloat16)
    decay_truncated = gradient_decay_low_rank.astype(jnp.bfloat16)
    rate_truncated = gradient_rate_low_rank.astype(jnp.bfloat16)
    value_low_rank_truncated = gradient_value_low_rank.astype(jnp.bfloat16)
    gate_round = grad_gate.astype(jnp.bfloat16)
    grad_upper = jnp.concatenate(
        [
            weight_grad(decay_truncated, decay_hidden),
            weight_grad(rate_truncated, rate_hidden),
            weight_grad(value_low_rank_truncated, value_hidden),
            weight_grad(gate_round, gate_hid),
        ],
        axis=1,
    )
    mix_sum = halve_sum(
        jnp.concatenate(
            [
                weight_grad(recv_in, recv_round),
                weight_grad(key_in, key_round),
                weight_grad(value_input, value_round),
                halves_side_by_side(grad_upper, half),
            ],
            axis=1,
        ),
        jnp.bfloat16,
        (0, 1, 3, 2),
    )
    part_hidden = jnp.concatenate(
        [
            product_matrix(decay_truncated, up_turned[:, :first_boundary]),
            product_matrix(rate_truncated, up_turned[:, first_boundary:second_boundary]),
            product_matrix(
                value_low_rank_truncated, up_turned[:, second_boundary:third_boundary]
            ),
            product_matrix(gate_round, up_turned[:, third_boundary:]),
        ],
        axis=1,
    )
    part_recv = back_product(recv_round, mix_full[0])
    part_key = back_product(key_round, mix_full[1])
    part_value = back_product(value_round, mix_full[2])
    hidden_sum = swap_sum(part_hidden)
    grad_recv_in = swap_sum(part_recv)
    grad_key_in = swap_sum(part_key)
    grad_value_part = swap_sum(part_value)
    tanh_decay = jnp.tanh(decay_lowrank_output)
    decay_low_round = (hidden_sum[:, :first_boundary] * (1.0 - tanh_decay * tanh_decay)).astype(
        jnp.bfloat16
    )
    rate_low_round = hidden_sum[:, first_boundary:second_boundary].astype(jnp.bfloat16)
    value_low_round = hidden_sum[:, second_boundary:third_boundary].astype(jnp.bfloat16)
    gate_low_round = (hidden_sum[:, third_boundary:] * gate_sig * (1.0 - gate_sig)).astype(
        jnp.bfloat16
    )
    grad_down = jnp.concatenate(
        [
            weight_grad(decay_input, decay_low_round),
            weight_grad(rate_input, rate_low_round),
            weight_grad(value_input, value_low_round),
            weight_grad(gate_input, gate_low_round),
        ],
        axis=1,
    )
    grad_decay_in = back_product(decay_low_round, down_full[:, :first_boundary])
    grad_rate_in = back_product(rate_low_round, down_full[:, first_boundary:second_boundary])
    grad_value_in = grad_value_part + back_product(
        value_low_round, down_full[:, second_boundary:third_boundary]
    )
    grad_gate_in = back_product(gate_low_round, down_full[:, third_boundary:])
    mix_grads = (
        grad_recv_in,
        grad_decay_in,
        grad_key_in,
        grad_value_in,
        grad_rate_in,
        grad_gate_in,
    )
    grad_coeffs = jnp.stack([jnp.sum(gradient * shift_one, axis=0) for gradient in mix_grads])
    direct_one = mix_grads[0] * (1.0 - chan_vals[4])
    toward_one = mix_grads[0] * chan_vals[4]
    for number in range(1, 6):
        direct_one = direct_one + mix_grads[number] * (1.0 - chan_vals[4 + number])
        toward_one = toward_one + mix_grads[number] * chan_vals[4 + number]
    toward_one = toward_one * keep_token[:, None]
    back_one = from_behind(toward_one[:1], "seq", -1)
    grad_norm_one = direct_one + jnp.concatenate([toward_one[1:], back_one], axis=0)
    grad_input, grad_gain_one, grad_bias_one = norm_one_pull(grad_norm_one)
    grad_input = grad_input + grad_hidden
    grad_chan = jnp.concatenate(
        [
            jnp.stack([grad_gain_one, grad_bias_one, grad_gain_two, grad_bias_two]),
            grad_coeffs,
            grad_coeff_two[None],
        ],
        axis=0,
    )
    grad_head = grad_head_a + grad_head_b
    small_sum = halve_sum(
        jnp.concatenate([grad_chan.T, halves_side_by_side(grad_head.T, half)], axis=1),
        jnp.float32,
        (1, 0, 3, 2),
    )
    chan_rows = grad_chan.shape[0]
    down_sum = halve_sum(grad_down, jnp.bfloat16, (1, 0, 3, 2))
    up_sum = halves_stacked(mix_sum[:, 3 * hidden_local :], half)
    return (
        block_out.astype(jnp.bfloat16),
        grad_input,
        grad_first,
        small_sum[:, :chan_rows].T,
        halves_stacked(small_sum[:, chan_rows:], half).T,
        jnp.stack(
            [
                mix_sum[:, number * hidden_local : (number + 1) * hidden_local]
                for number in range(3)
            ]
        ),
        out_sum.T,
        down_sum,
        up_sum.T,
        key_sum,
        value_sum.T,
    )


def solution(mesh):
    in_specs = (
        P("seq", None),
        P("seq", "head"),
        P("seq", None),
        P(),
        P(None, "seq"),
        P(None, ("head", "seq")),
        P(None, "seq", "head"),
        P("head", "seq"),
        P("seq", None),
        P(None, ("head", "seq")),
        P("seq", "head"),
        P("head", "seq"),
    )
    out_specs = (
        P("seq", None),
        P("seq", None),
        P("seq", "head"),
        P(None, "seq"),
        P(None, ("head", "seq")),
        P(None, "seq", "head"),
        P("head", "seq"),
        P("seq", None),
        P(None, ("head", "seq")),
        P("seq", "head"),
        P("head", "seq"),
    )
    return jax.shard_map(shards, mesh=mesh, in_specs=in_specs, out_specs=out_specs, check_vma=False)
```

```python
from functools import partial

import jax
import jax.numpy as jnp
from jax import lax
from jax.sharding import PartitionSpec as P

ATTEND_DIM = 64
DECAY_LOW_RANK = 64
RATE_RANK = 64
VALUE_RANK = 32
BLK = 16


PRECISE = lax.Precision.HIGHEST
FINE = lax.Precision.HIGH


def from_behind(value, axis, steps):
    count = lax.axis_size(axis)
    initial, last = (max(0, -steps), min(count, count - steps))
    return lax.ppermute(value, axis, [(source, source + steps) for source in range(initial, last)])


def swap_sum(value):
    return value + lax.ppermute(value, "head", [(0, 1), (1, 0)])


def times(left, right, turned=False):
    shape = "hij,hkj->hik" if turned else "hij,hjk->hik"
    return jnp.einsum(shape, left, right, precision=FINE)


def chain_steps(count):
    return [1 << power for power in range((count - 1).bit_length())]


def exclusive_chain(own_map, own_add, direction):
    count = lax.axis_size("seq")
    place = lax.axis_index("seq")
    behind = place if direction > 0 else count - 1 - place
    width = own_map.shape[1]
    total = jnp.concatenate([jnp.swapaxes(own_map, 1, 2), jnp.swapaxes(own_add, 1, 2)], axis=2)
    from_map = (jnp.arange(2 * width) < width)[None, None]
    for step in chain_steps(count):
        arrived = from_behind(total, "seq", direction * step)
        moved = times(total[:, :, :width], arrived)
        total = jnp.where(from_map & (behind >= step), 0.0, total) + jnp.where(
            from_map & (behind < step), 0.0, moved
        )
    return jnp.swapaxes(from_behind(total[:, :, width:], "seq", direction), 1, 2)


def halve_order(first):
    bits = (lax.axis_size("seq") - 1).bit_length()
    order = list(range(bits))
    return order[first::-1] + order[first + 1 :]


def halve_start(rows):
    count = lax.axis_size("seq")
    bits = (count - 1).bit_length()
    return rows.reshape((2,) * bits + (rows.shape[0] // count, rows.shape[1]))


def halve_step(held, order, number, sent_type, after=None):
    count = lax.axis_size("seq")
    bit = order[number]
    where = sorted(order[number:], reverse=True).index(bit)
    mine = (lax.axis_index("seq") >> bit) & 1
    kept = lax.dynamic_index_in_dim(held, mine, where, False)
    sent = lax.dynamic_index_in_dim(held, 1 - mine, where, False)
    if after is not None:
        sent = sent + after
    pairs = [(place, place ^ (1 << bit)) for place in range(count)]
    arrived = lax.ppermute(sent.astype(sent_type), "seq", pairs)
    return kept.astype(jnp.float32) + arrived.astype(jnp.float32)


def halve_sum(rows, sent_type, first, after=None):
    order = halve_order(first)
    held = halve_start(rows)
    for number in range(len(order)):
        held = halve_step(held, order, number, sent_type, after if number == 0 else None)
    return held


def order_mark(value):
    return value[(0,) * value.ndim].astype(jnp.float32) * 0.0


def halves_side_by_side(rows, width):
    columns = rows.shape[1] // 2
    cut = rows.reshape(-1, width, 2 * columns)
    return jnp.concatenate([cut[:, :, :columns], cut[:, :, columns:]], axis=1).reshape(-1, columns)


def halves_stacked(rows, width):
    columns = rows.shape[1]
    cut = rows.reshape(-1, 2 * width, columns)
    return jnp.concatenate([cut[:, :width], cut[:, width:]], axis=2).reshape(-1, 2 * columns)


def product_matrix(operand, weights):
    return jnp.dot(operand, weights, preferred_element_type=jnp.float32)


def back_product(gradient, weights):
    return lax.dot_general(
        gradient, weights, (((1,), (1,)), ((), ())), preferred_element_type=jnp.float32
    )


def weight_grad(operand, gradient):
    return lax.dot_general(
        operand, gradient, (((0,), (0,)), ((), ())), preferred_element_type=jnp.float32
    )


def layer_norm(value_rows, scale_vec, offset_vec):
    centre = value_rows - jnp.mean(value_rows, axis=-1, keepdims=True)
    spread = jnp.mean(centre * centre, axis=-1, keepdims=True)
    return centre * lax.rsqrt(spread + 1e-05) * scale_vec + offset_vec


def prepare_inputs(
    receptance_unscaled,
    key_unscaled,
    value_unscaled,
    decay_low_rank,
    rate_low_rank,
    value_low_rank,
    first_layer_value,
    attend_elements,
):
    rows_here = receptance_unscaled.shape[0]
    attend_count = receptance_unscaled.shape[1] // ATTEND_DIM
    logarithm_scale = -jax.nn.softplus(-(attend_elements[0] + decay_low_rank)) - 0.5
    log_decay = -jnp.exp(logarithm_scale)
    rate_sigmoid = jax.nn.sigmoid(attend_elements[1] + rate_low_rank)
    payload_blended = value_unscaled + (first_layer_value - value_unscaled) * jax.nn.sigmoid(
        attend_elements[2] + value_low_rank
    )
    scaled = (key_unscaled * attend_elements[3]).reshape(rows_here, attend_count, ATTEND_DIM)
    unit_key = scaled * lax.rsqrt(jnp.sum(scaled * scaled, axis=-1, keepdims=True) + 1e-05)
    lookup_used = key_unscaled * (1.0 + (rate_sigmoid - 1.0) * attend_elements[4])
    layout = (rows_here, attend_count, ATTEND_DIM)
    return (
        receptance_unscaled.reshape(layout),
        log_decay.reshape(layout),
        -unit_key,
        unit_key * rate_sigmoid.reshape(layout),
        lookup_used.reshape(layout),
        payload_blended.reshape(layout),
    )


def finish(
    read_out, reader_vectors, lookup_used, payload_blended, gate_activation, attend_elements
):
    rows_here, attend_count, _ = read_out.shape
    centre = read_out - jnp.mean(read_out, axis=-1, keepdims=True)
    unit_length_vectors = centre * lax.rsqrt(
        jnp.mean(centre * centre, axis=-1, keepdims=True) + 0.00064
    )
    extra_addend = (
        jnp.sum(
            reader_vectors * lookup_used * attend_elements[5].reshape(attend_count, ATTEND_DIM),
            axis=-1,
            keepdims=True,
        )
        * payload_blended
    )
    final_answer = (
        unit_length_vectors * attend_elements[6].reshape(attend_count, ATTEND_DIM)
        + attend_elements[7].reshape(attend_count, ATTEND_DIM)
        + extra_addend
    )
    return final_answer.reshape(rows_here, attend_count * ATTEND_DIM) * gate_activation


@jax.custom_vjp
def unit_inverse(strict_part):
    unit = jnp.eye(strict_part.shape[-1], dtype=jnp.float32)[None]
    inverse = unit + strict_part
    power = strict_part
    for _ in range(BLK.bit_length() - 2):
        power = times(power, power)
        inverse = inverse + times(inverse, power)
    return inverse


def unit_inverse_keep(strict_part):
    inverse = unit_inverse(strict_part)
    return inverse, inverse


def unit_inverse_pull(inverse, gradient):
    turned = jnp.swapaxes(inverse, 1, 2)
    return (times(times(turned, gradient), turned),)


unit_inverse.defvjp(unit_inverse_keep, unit_inverse_pull)


def chunk_terms(reader_vectors, log_decay, removal, refill, lookup_used, payload_blended, keep):
    rows_here, attend_count, head_width = reader_vectors.shape
    block_count = rows_here // BLK
    recv, decay, removal, refill, lookup, payload = [
        jnp.transpose(rows, (1, 0, 2))
        for rows in (reader_vectors, log_decay, removal, refill, lookup_used, payload_blended)
    ]
    token = jnp.arange(rows_here)
    same = (token[:, None] // BLK) == (token[None, :] // BLK)
    strict = (same & (token[:, None] > token[None, :])).astype(jnp.float32)
    inclusive = (same & (token[:, None] >= token[None, :])).astype(jnp.float32)

    def blocks(rows):
        return rows.reshape(attend_count, block_count, BLK, head_width)

    cumulative = jnp.einsum("ts,hsj->htj", inclusive, decay, precision=PRECISE)
    growth = jnp.exp(-cumulative)
    refill_grown = refill * growth
    key_grown = lookup * growth
    first_term = removal * jnp.exp(cumulative - decay)
    reader_term = recv * jnp.exp(cumulative)
    mix_refill = times(first_term, refill_grown, True) * strict
    mix_key = times(first_term, key_grown, True) * strict
    read_refill = times(reader_term, refill_grown, True) * inclusive
    read_key = times(reader_term, key_grown, True) * inclusive
    inverse = unit_inverse(mix_refill)
    removed_map = times(inverse, first_term)
    removed_add = times(inverse, times(mix_key, payload))
    read_map = reader_term + times(read_refill, removed_map)
    read_add = times(read_refill, removed_add) + times(read_key, payload)
    total = blocks(cumulative)[:, :, BLK - 1 :]
    tail = jnp.exp(total - blocks(cumulative))
    refill_tail = blocks(refill) * tail
    key_tail = blocks(lookup) * tail

    def outer(left, right):
        return jnp.einsum("hcti,hctj->chij", blocks(left), right, precision=FINE)

    unit = jnp.eye(head_width, dtype=jnp.float32)
    kept = keep[:, None, None, None]
    decayed = jnp.exp(jnp.transpose(total, (1, 0, 2, 3)))
    state_map = (unit * decayed + outer(removed_map, refill_tail)) * kept
    state_add = outer(removed_add, refill_tail) + outer(payload, key_tail)
    return state_map, state_add, blocks(read_map) * keep[None, :, None, None], read_add


def shards(
    block_input,
    first_layer_value,
    output_gradient,
    segment_index,
    channel_parameters,
    head_parameters,
    mixing_weights,
    output_weight,
    low_rank_down_weight,
    low_rank_up_weight,
    channel_key_matrix,
    channel_value_matrix,
):
    width = low_rank_down_weight.shape[0]
    half = low_rank_up_weight.shape[1]
    hidden_local = mixing_weights.shape[2]
    low_columns = low_rank_down_weight.shape[1]
    head_rows = head_parameters.shape[0]
    own_columns = jnp.concatenate([low_rank_up_weight, head_parameters], axis=0).T
    first_pack = jnp.concatenate(
        [
            mixing_weights[0],
            mixing_weights[1],
            mixing_weights[2],
            low_rank_down_weight,
            halves_side_by_side(own_columns, half),
            channel_parameters.T,
        ],
        axis=1,
    )
    first_full = lax.all_gather(first_pack, "seq", axis=0, tiled=True)
    later_pack = jnp.concatenate(
        [output_weight.T, channel_key_matrix, channel_value_matrix.T], axis=1
    )
    later_full = lax.all_gather(later_pack, "seq", axis=0, tiled=True)
    mix_full = [
        first_full[:, number * hidden_local : (number + 1) * hidden_local] for number in range(3)
    ]
    place_down = 3 * hidden_local
    place_up = place_down + low_columns
    place_chan = place_up + (low_columns + head_rows) // 2
    down_full = first_full[:, place_down:place_up]
    columns_full = halves_stacked(first_full[:, place_up:place_chan], half)
    up_turned = columns_full[:, :low_columns]
    head_full = columns_full[:, low_columns:].T
    chan_full = first_full[:, place_chan:].T
    units = channel_key_matrix.shape[1]
    out_turned = later_full[:, :hidden_local]
    key_full = later_full[:, hidden_local : hidden_local + units]
    value_turned = later_full[:, hidden_local + units :]
    chan_vals = chan_full.astype(jnp.float32)
    attend_elements = head_full.astype(jnp.float32)
    first_boundary = DECAY_LOW_RANK
    second_boundary = first_boundary + RATE_RANK
    third_boundary = second_boundary + VALUE_RANK
    rows_here = block_input.shape[0]
    attend_count = head_full.shape[1] // ATTEND_DIM
    block_count = rows_here // BLK
    place = lax.axis_index("seq")
    earlier_id = jnp.where(
        place > 0,
        lax.dynamic_slice_in_dim(segment_index, jnp.maximum(place * block_count - 1, 0), 1),
        -1,
    )
    own_ids = lax.dynamic_slice_in_dim(segment_index, place * block_count, block_count)
    block_starts = (own_ids != jnp.concatenate([earlier_id, own_ids[:-1]])).astype(jnp.float32)
    keep_block = 1.0 - block_starts
    keep_token = jnp.concatenate(
        [keep_block[:, None], jnp.ones((block_count, BLK - 1), jnp.float32)], axis=1
    ).reshape(-1)
    x_input = block_input.astype(jnp.float32)
    norm_one, norm_one_pull = jax.vjp(layer_norm, x_input, chan_vals[0], chan_vals[1])
    edge_one = from_behind(norm_one[rows_here - 1 :], "seq", 1)
    shift_one = jnp.concatenate([edge_one, norm_one[:-1]], axis=0) * keep_token[:, None] - norm_one
    recv_in, decay_input, key_in, value_input, rate_input, gate_input = [
        (norm_one + shift_one * chan_vals[4 + number]).astype(jnp.bfloat16) for number in range(6)
    ]
    receptance_unscaled = product_matrix(recv_in, mix_full[0])
    key_unscaled = product_matrix(key_in, mix_full[1])
    value_unscaled = product_matrix(value_input, mix_full[2])
    decay_lowrank_output = product_matrix(decay_input, down_full[:, :first_boundary])
    rate_lowrank_output = product_matrix(rate_input, down_full[:, first_boundary:second_boundary])
    value_lowrank_output = product_matrix(value_input, down_full[:, second_boundary:third_boundary])
    gate_lowrank_output = product_matrix(gate_input, down_full[:, third_boundary:])
    decay_hidden = jnp.tanh(decay_lowrank_output).astype(jnp.bfloat16)
    rate_hidden = rate_lowrank_output.astype(jnp.bfloat16)
    value_hidden = value_lowrank_output.astype(jnp.bfloat16)
    gate_sig = jax.nn.sigmoid(gate_lowrank_output)
    gate_hid = gate_sig.astype(jnp.bfloat16)
    decay_low_rank = back_product(decay_hidden, up_turned[:, :first_boundary])
    rate_low_rank = back_product(rate_hidden, up_turned[:, first_boundary:second_boundary])
    value_low_rank = back_product(
        value_hidden, up_turned[:, second_boundary:third_boundary]
    )
    gate_activation = back_product(gate_hid, up_turned[:, third_boundary:])
    first_values = first_layer_value.astype(jnp.float32)
    prepared_inputs, prepare_pull = jax.vjp(
        prepare_inputs,
        receptance_unscaled,
        key_unscaled,
        value_unscaled,
        decay_low_rank,
        rate_low_rank,
        value_low_rank,
        first_values,
        attend_elements,
    )
    (state_map, state_add, read_map, read_add), local_pull = jax.vjp(
        partial(chunk_terms, keep=keep_block), *prepared_inputs
    )
    before_map, before_add = [None], [None]
    run_map, run_add = state_map[0], state_add[0]
    for number in range(1, block_count):
        before_map.append(run_map)
        before_add.append(run_add)
        run_add = times(run_add, state_map[number]) + state_add[number]
        run_map = times(run_map, state_map[number])
    after_map = [state_map[block_count - 1]]
    for number in range(block_count - 2, -1, -1):
        after_map.append(times(state_map[number], after_map[-1]))
    after_map = after_map[::-1]
    start_state = exclusive_chain(run_map, run_add, 1)
    states = jnp.concatenate(
        [
            start_state[None],
            jnp.einsum("hij,chjk->chik", start_state, jnp.stack(before_map[1:]), precision=FINE)
            + jnp.stack(before_add[1:]),
        ],
        axis=0,
    )
    read_out = jnp.transpose(
        jnp.einsum("hctj,chij->hcti", read_map, states, precision=FINE).reshape(read_add.shape)
        + read_add,
        (1, 0, 2),
    )
    mixed_f, finish_pull = jax.vjp(
        finish,
        read_out,
        prepared_inputs[0],
        prepared_inputs[4],
        prepared_inputs[5],
        gate_activation,
        attend_elements,
    )
    mixed_low = mixed_f.astype(jnp.bfloat16)
    hidden_in = x_input + swap_sum(back_product(mixed_low, out_turned))
    norm_two, norm_two_pull = jax.vjp(layer_norm, hidden_in, chan_vals[2], chan_vals[3])
    edge_two = from_behind(norm_two[rows_here - 1 :], "seq", 1)
    shift_two = jnp.concatenate([edge_two, norm_two[:-1]], axis=0) * keep_token[:, None] - norm_two
    key_two = (norm_two + shift_two * chan_vals[10]).astype(jnp.bfloat16)
    pre_act = product_matrix(key_two, key_full)
    activated = jnp.square(jax.nn.relu(pre_act)).astype(jnp.bfloat16)
    block_out = hidden_in + swap_sum(back_product(activated, value_turned))
    grad_output = output_gradient.astype(jnp.float32)
    grad_ffo = grad_output.astype(jnp.bfloat16)
    value_held = halve_start(weight_grad(grad_ffo, activated))
    grad_pre = (product_matrix(grad_ffo, value_turned) * 2.0 * jax.nn.relu(pre_act)).astype(
        jnp.bfloat16
    )
    key_held = halve_start(weight_grad(key_two, grad_pre))
    part_key_two = back_product(grad_pre, key_full)
    grad_key_two = swap_sum(part_key_two)
    grad_coeff_two = jnp.sum(grad_key_two * shift_two, axis=0)
    toward_two = grad_key_two * chan_vals[10] * keep_token[:, None]
    back_two = from_behind(toward_two[:1], "seq", -1)
    key_order, value_order = halve_order(0), halve_order(1)
    edge_mark = order_mark(back_two)
    key_held = halve_step(key_held, key_order, 0, jnp.bfloat16, edge_mark)
    value_held = halve_step(value_held, value_order, 0, jnp.bfloat16, edge_mark)
    grad_norm_two = grad_key_two * (1.0 - chan_vals[10]) + jnp.concatenate(
        [toward_two[1:], back_two], axis=0
    )
    grad_hidden, grad_gain_two, grad_bias_two = norm_two_pull(grad_norm_two)
    grad_hidden = grad_hidden + grad_output
    grad_attn = grad_hidden.astype(jnp.bfloat16)
    grad_out_turned = weight_grad(grad_attn, mixed_low)
    grad_mixed = product_matrix(grad_attn, out_turned)
    grad_read, grad_recv_a, grad_key_a, grad_value_a, grad_gate, grad_head_a = finish_pull(
        grad_mixed
    )
    read_turned = jnp.transpose(grad_read, (1, 0, 2))
    read_blocks = read_turned.reshape(read_map.shape)
    grad_states = jnp.einsum("hcti,hctj->chij", read_blocks, read_map, precision=FINE)
    run_grad = grad_states[block_count - 1]
    after_grad = [jnp.zeros_like(run_grad), run_grad]
    for number in range(block_count - 2, -1, -1):
        run_grad = grad_states[number] + times(run_grad, state_map[number], True)
        after_grad.append(run_grad)
    after_grad = jnp.stack(after_grad[block_count - 1 :: -1])
    grad_end = exclusive_chain(jnp.swapaxes(run_map, 1, 2), run_grad, -1)
    grad_add = after_grad + jnp.concatenate(
        [
            jnp.einsum("hij,chkj->chik", grad_end, jnp.stack(after_map[1:]), precision=FINE),
            grad_end[None],
        ],
        axis=0,
    )
    grad_map = jnp.einsum("chij,chik->chjk", states, grad_add, precision=FINE)
    grad_read_map = jnp.einsum("hcti,chij->hctj", read_blocks, states, precision=FINE)
    chain_grads = local_pull((grad_map, grad_add, grad_read_map, read_turned))
    cotangents = (
        grad_recv_a + chain_grads[0],
        chain_grads[1],
        chain_grads[2],
        chain_grads[3],
        grad_key_a + chain_grads[4],
        grad_value_a + chain_grads[5],
    )
    (
        grad_recv_raw,
        grad_key_raw,
        grad_value_raw,
        gradient_decay_low_rank,
        gradient_rate_low_rank,
        gradient_value_low_rank,
        grad_first,
        grad_head_b,
    ) = prepare_pull(cotangents)
    recv_round = grad_recv_raw.astype(jnp.bfloat16)
    key_round = grad_key_raw.astype(jnp.bfloat16)
    value_round = grad_value_raw.astype(jnp.bfloat16)
    decay_truncated = gradient_decay_low_rank.astype(jnp.bfloat16)
    rate_truncated = gradient_rate_low_rank.astype(jnp.bfloat16)
    value_low_rank_truncated = gradient_value_low_rank.astype(jnp.bfloat16)
    gate_round = grad_gate.astype(jnp.bfloat16)
    grad_upper = jnp.concatenate(
        [
            weight_grad(decay_truncated, decay_hidden),
            weight_grad(rate_truncated, rate_hidden),
            weight_grad(value_low_rank_truncated, value_hidden),
            weight_grad(gate_round, gate_hid),
        ],
        axis=1,
    )
    mix_sum = halve_sum(
        jnp.concatenate(
            [
                weight_grad(recv_in, recv_round),
                weight_grad(key_in, key_round),
                halves_side_by_side(grad_upper, half),
            ],
            axis=1,
        ),
        jnp.bfloat16,
        0,
    )
    rest_sum = halve_sum(
        jnp.concatenate([weight_grad(value_input, value_round), grad_out_turned], axis=1),
        jnp.bfloat16,
        1,
    )
    for number in range(1, len(key_order)):
        key_held = halve_step(key_held, key_order, number, jnp.bfloat16)
        value_held = halve_step(value_held, value_order, number, jnp.bfloat16)
    part_hidden = jnp.concatenate(
        [
            product_matrix(decay_truncated, up_turned[:, :first_boundary]),
            product_matrix(rate_truncated, up_turned[:, first_boundary:second_boundary]),
            product_matrix(
                value_low_rank_truncated, up_turned[:, second_boundary:third_boundary]
            ),
            product_matrix(gate_round, up_turned[:, third_boundary:]),
        ],
        axis=1,
    )
    part_recv = back_product(recv_round, mix_full[0])
    part_key = back_product(key_round, mix_full[1])
    part_value = back_product(value_round, mix_full[2])
    hidden_sum = swap_sum(part_hidden)
    grad_recv_in = swap_sum(part_recv)
    grad_key_in = swap_sum(part_key)
    grad_value_part = swap_sum(part_value)
    tanh_decay = jnp.tanh(decay_lowrank_output)
    decay_low_round = (hidden_sum[:, :first_boundary] * (1.0 - tanh_decay * tanh_decay)).astype(
        jnp.bfloat16
    )
    rate_low_round = hidden_sum[:, first_boundary:second_boundary].astype(jnp.bfloat16)
    value_low_round = hidden_sum[:, second_boundary:third_boundary].astype(jnp.bfloat16)
    gate_low_round = (hidden_sum[:, third_boundary:] * gate_sig * (1.0 - gate_sig)).astype(
        jnp.bfloat16
    )
    grad_down = jnp.concatenate(
        [
            weight_grad(decay_input, decay_low_round),
            weight_grad(rate_input, rate_low_round),
            weight_grad(value_input, value_low_round),
            weight_grad(gate_input, gate_low_round),
        ],
        axis=1,
    )
    grad_decay_in = back_product(decay_low_round, down_full[:, :first_boundary])
    grad_rate_in = back_product(rate_low_round, down_full[:, first_boundary:second_boundary])
    grad_value_in = grad_value_part + back_product(
        value_low_round, down_full[:, second_boundary:third_boundary]
    )
    grad_gate_in = back_product(gate_low_round, down_full[:, third_boundary:])
    mix_grads = (
        grad_recv_in,
        grad_decay_in,
        grad_key_in,
        grad_value_in,
        grad_rate_in,
        grad_gate_in,
    )
    grad_coeffs = jnp.stack([jnp.sum(gradient * shift_one, axis=0) for gradient in mix_grads])
    direct_one = mix_grads[0] * (1.0 - chan_vals[4])
    toward_one = mix_grads[0] * chan_vals[4]
    for number in range(1, 6):
        direct_one = direct_one + mix_grads[number] * (1.0 - chan_vals[4 + number])
        toward_one = toward_one + mix_grads[number] * chan_vals[4 + number]
    toward_one = toward_one * keep_token[:, None]
    back_one = from_behind(toward_one[:1], "seq", -1)
    grad_norm_one = direct_one + jnp.concatenate([toward_one[1:], back_one], axis=0)
    grad_input, grad_gain_one, grad_bias_one = norm_one_pull(grad_norm_one)
    grad_input = grad_input + grad_hidden
    grad_chan = jnp.concatenate(
        [
            jnp.stack([grad_gain_one, grad_bias_one, grad_gain_two, grad_bias_two]),
            grad_coeffs,
            grad_coeff_two[None],
        ],
        axis=0,
    )
    grad_head = grad_head_a + grad_head_b
    small_sum = halve_sum(
        jnp.concatenate([grad_down, grad_chan.T, halves_side_by_side(grad_head.T, half)], axis=1),
        jnp.float32,
        1,
    )
    place_head = low_columns + grad_chan.shape[0]
    up_sum = halves_stacked(mix_sum[:, 2 * hidden_local :], half)
    return (
        block_out.astype(jnp.bfloat16),
        grad_input,
        grad_first,
        small_sum[:, low_columns:place_head].T,
        halves_stacked(small_sum[:, place_head:], half).T,
        jnp.stack(
            [
                mix_sum[:, :hidden_local],
                mix_sum[:, hidden_local : 2 * hidden_local],
                rest_sum[:, :hidden_local],
            ]
        ),
        rest_sum[:, hidden_local:].T,
        small_sum[:, :low_columns],
        up_sum.T,
        key_held,
        value_held.T,
    )


def solution(mesh):
    in_specs = (
        P("seq", None),
        P("seq", "head"),
        P("seq", None),
        P(),
        P(None, "seq"),
        P(None, ("head", "seq")),
        P(None, "seq", "head"),
        P("head", "seq"),
        P("seq", None),
        P(None, ("head", "seq")),
        P("seq", "head"),
        P("head", "seq"),
    )
    out_specs = (
        P("seq", None),
        P("seq", None),
        P("seq", "head"),
        P(None, "seq"),
        P(None, ("head", "seq")),
        P(None, "seq", "head"),
        P("head", "seq"),
        P("seq", None),
        P(None, ("head", "seq")),
        P("seq", "head"),
        P("head", "seq"),
    )
    return jax.shard_map(shards, mesh=mesh, in_specs=in_specs, out_specs=out_specs, check_vma=False)
```
